32 devices in a mesh: grp: 2 (over y), seq: 16 (over z, x, core).
Axes of the slice: x: 2, y: 2, z: 4, core: 2. Of those that a mesh axis runs over, the one named last changes fastest.
Arguments:
- queries: bfloat16 [4096, 768], P(('grp', 'seq')), parts along dimension 0, may hold values from -2.5 to 2.5
- key_rows: bfloat16 [4096, 768], P(('grp', 'seq')), parts along dimension 0, may hold values from -2.5 to 2.5
- value_rows: bfloat16 [4096, 768], P(('grp', 'seq')), parts along dimension 0, may hold values from -6 to 6
- out_grad: bfloat16 [4096, 768], P(('grp', 'seq')), parts along dimension 0, may hold values from -6 to 6
- ssm_input: bfloat16 [4096, 768], P(('grp', 'seq')), parts along dimension 0, may hold values from -0.125 to 0.125
- state_write: bfloat16 [4096, 128], P(('grp', 'seq')), parts along dimension 0, may hold values from -0.1875 to 0.1875
- state_read: bfloat16 [4096, 128], P(('grp', 'seq')), parts along dimension 0, may hold values from -0.1875 to 0.1875
- log_decay: float32 [12, 4096], P(None, ('grp', 'seq')), parts along dimension 1, may hold values from -0.8 to 0, as said below
- block_lists: int32 [32, 4], P(('grp', 'seq')), parts along dimension 0, may hold values from -1 to 15, as said below
- rec_lengths: int32 [16], P('grp'), parts along dimension 0, may hold values from 1 to 1024, 2048 in all
Outputs:
- grad_queries: bfloat16 [4096, 768], P(('grp', 'seq')), parts along dimension 0
- grad_keys: bfloat16 [4096, 768], P(('grp', 'seq')), parts along dimension 0
- grad_values: bfloat16 [4096, 768], P(('grp', 'seq')), parts along dimension 0
- grad_input: bfloat16 [4096, 768], P(('grp', 'seq')), parts along dimension 0
- grad_write: bfloat16 [4096, 128], P(('grp', 'seq')), parts along dimension 0
- grad_read: bfloat16 [4096, 128], P(('grp', 'seq')), parts along dimension 0
- grad_decay: float32 [12, 4096], P(None, ('grp', 'seq')), parts along dimension 1
The draws below stay inside these ranges and needn't reach their ends.
There are 2 independent parts, one for each index of `grp`. The reference program is written for one: setup_inputs(seed, part) draws one part's arguments, and reference() takes and returns one part's arrays. A program takes and returns all parts, laid end to end along the dimension named above; each array names one. Nothing has to cross between parts.
Inputs may be any that keep to these rules, and one draw needn't show every extreme that they name: `block_lists`: entry 0 of row b is b itself; the other 3 entries are distinct blocks 1 to 4 blocks before b, each replaced by -1 where it would be negative. `log_decay`: all log-decays are negative.
All inputs are finite; a program needn't handle non-finite values.
Results may differ from the reference program's by a relative error of at most 0.0057.
Values may be sent and summed in bfloat16 or wider, within the bound.
A program may use at most 256 MiB of HBM per device.

```python
import math
import jax
import jax.numpy as jnp
import numpy as np
from jax import lax

ATTENDER_COUNT = 12
D = 768
NSTATE = 128
BLOCK = 128
KSEL = 4
REC = 8
TOK_DEV = 128
SPAN_STEPS = 2048
QBLOCKS = 16
KWIN = 4


def draw_log_decay(key, part):
    complete_lookup_lines = jax.random.split(key, 6)
    slow_share = 0.5
    slow_pick = jax.random.uniform(complete_lookup_lines[0], (ATTENDER_COUNT,)) < slow_share
    fast_rate = jnp.exp(jax.random.uniform(complete_lookup_lines[1], (ATTENDER_COUNT,), minval=jnp.log(1.0 / 50.0), maxval=jnp.log(1.0 / 30.0)))
    slow_rate = jnp.exp(jax.random.uniform(complete_lookup_lines[2], (ATTENDER_COUNT,), minval=jnp.log(0.05 / SPAN_STEPS), maxval=jnp.log(0.5 / SPAN_STEPS)))
    fading_rate = jnp.where(slow_pick, slow_rate, fast_rate)
    scaling_factor = jnp.exp(jax.random.uniform(complete_lookup_lines[3], (ATTENDER_COUNT, SPAN_STEPS), minval=jnp.log(0.5), maxval=jnp.log(2.0)))
    spurt_offset = jax.random.uniform(complete_lookup_lines[4], (SPAN_STEPS,)) < 2.0 / SPAN_STEPS
    spurt_extent = jnp.log(jax.random.uniform(complete_lookup_lines[5], (ATTENDER_COUNT, SPAN_STEPS), minval=0.5, maxval=0.8))
    ultimate_result = -fading_rate[:, None] * scaling_factor + jnp.where(spurt_offset[None, :], spurt_extent, 0.0)
    return ultimate_result.astype(jnp.float32)


def draw_block_lists(key, part):
    row_keys = jax.random.split(key, QBLOCKS)
    offsets = jax.vmap(lambda row_key: jax.random.permutation(row_key, KWIN))(row_keys)[:, :KSEL - 1] + 1
    own_block = jnp.arange(QBLOCKS, dtype=jnp.int32)[:, None]
    earlier = own_block - offsets.astype(jnp.int32)
    earlier = jnp.where(earlier >= 0, earlier, -1)
    return jnp.concatenate([own_block, earlier], axis=1).astype(jnp.int32)


def shard_levels(key, shape, shards, least, high):
    def one(dim, shards_of):
        heights = jax.random.uniform(jax.random.fold_in(jax.random.fold_in(key, 6), dim), (shards_of,), jnp.float32, least / len(shards), high / len(shards))
        return jnp.repeat(jnp.exp(heights), shape[dim] // shards_of).reshape((-1,) + (1,) * (len(shape) - dim - 1))

    loudness = one(*shards[0])
    for cut in shards[1:]:
        loudness = loudness * one(*cut)
    return loudness


def profile(count, total, reach, skew):
    portions = [(1 << 20) // math.isqrt(grade ** skew) + 1 for grade in range(2, count + 1)]
    surplus, counts = total - reach - (count - 1), [1] * (count - 1)
    while surplus > 0:
        candidates = [i for i in range(count - 1) if counts[i] < reach]
        whole, budget = sum([portions[i] for i in candidates]), surplus
        for i in candidates:
            addition = min(reach - counts[i], max(1, budget * portions[i] // whole), surplus)
            counts[i] = counts[i] + addition
            surplus = surplus - addition
    return np.array([reach] + counts)


def uneven_parts(key, number_of, total, bound, lean):
    if number_of == 2:
        one = jax.random.randint(key, (), max(1, total - bound), min(bound, total - 1) + 1)
        return jnp.stack([one, total - one])
    sizes = jnp.asarray(profile(number_of, total, bound, lean), jnp.int32)
    twos = (number_of - 1) // 2
    donor, sink = sizes[1:1 + 2 * twos:2], sizes[2:2 + 2 * twos:2]
    room = jnp.minimum(donor - 1, bound - sink)
    passed = jax.random.randint(jax.random.fold_in(key, 1), (twos,), 0, 1 << 20) % (room + 1)
    sizes = sizes.at[1:1 + 2 * twos:2].set(donor - passed).at[2:2 + 2 * twos:2].set(sink + passed)
    return sizes[jax.random.permutation(jax.random.fold_in(key, 2), number_of)]


def centred(own_key, extent, width, most, cuts=(), kind=jnp.bfloat16):
    gain = shard_levels(own_key, extent, cuts, -0.22, 0.18) if cuts else 1.0
    result = jax.random.normal(own_key, extent, jnp.float32) * width * gain
    return jnp.minimum(jnp.maximum(result, -most), most).astype(kind)


def setup_inputs(seed: int = 0, part: int = 0) -> dict:
    streams_of = jax.random.split(jax.random.key(seed), 11)
    own_keys = jax.random.split(jax.random.fold_in(streams_of[10], part), 11)
    return {
        "queries": centred(own_keys[0], (SPAN_STEPS, D), 1.0, 2.5, ((0, 16),)),
        "key_rows": centred(own_keys[1], (SPAN_STEPS, D), 1.0, 2.5, ((0, 16),)),
        "value_rows": centred(own_keys[2], (SPAN_STEPS, D), 1.0, 6.0, ((0, 16),)),
        "out_grad": centred(own_keys[3], (SPAN_STEPS, D), 1.0, 6.0, ((0, 16),)),
        "ssm_input": centred(own_keys[4], (SPAN_STEPS, D), 0.02, 0.125, ((0, 16),)),
        "state_write": centred(own_keys[5], (SPAN_STEPS, NSTATE), 0.03, 0.1875, ((0, 16),)),
        "state_read": centred(own_keys[6], (SPAN_STEPS, NSTATE), 0.03, 0.1875, ((0, 16),)),
        "log_decay": draw_log_decay(jax.random.fold_in(jax.random.fold_in(streams_of[10], part), 71), part),
        "block_lists": draw_block_lists(jax.random.fold_in(jax.random.fold_in(streams_of[10], part), 71), part),
        "rec_lengths": uneven_parts(own_keys[9], REC, SPAN_STEPS, SPAN_STEPS // 2, 2).astype(jnp.int32),
    }


PRECISE = lax.Precision.HIGHEST


def recording_of(positions, rec_lengths):
    boundary = jnp.cumsum(rec_lengths).astype(jnp.int32)
    return jnp.sum((positions[..., None] >= boundary).astype(jnp.int32), axis=-1)


def keep_of(positions, rec_lengths):
    boundary = jnp.cumsum(rec_lengths).astype(jnp.int32)
    opening = jnp.any(positions[..., None] == boundary, axis=-1) | (positions == 0)
    return jnp.where(opening, 0.0, 1.0).astype(jnp.float32)


def piece_setup(decay_part, keep_part, rec_part):
    span_len = decay_part.shape[-1]
    upper_tri = jnp.arange(span_len)[:, None] >= jnp.arange(span_len)[None, :]
    cumulative = jnp.cumsum(decay_part, axis=-1)
    spread = cumulative[..., :, None] - cumulative[..., None, :]
    same_rec = rec_part[:, :, None] == rec_part[:, None, :]
    live_pair = (upper_tri[None] & same_rec)[:, None]
    lower_mat = jnp.where(live_pair, jnp.exp(jnp.where(live_pair, spread, 0.0)), 0.0)
    head_live = keep_part[:, :1] * (rec_part == rec_part[:, :1]).astype(decay_part.dtype)
    enter_w = jnp.exp(cumulative) * head_live[:, None, :]
    tail_live = (rec_part == rec_part[:, -1:]).astype(decay_part.dtype)
    leave_w = jnp.exp(cumulative[..., -1:] - cumulative) * tail_live[:, None, :]
    return lower_mat, enter_w, leave_w


def piece_summary(input_part, write_part, read_part, grad_part, enter_w, leave_w):
    through = enter_w[..., -1]
    pushed = jnp.einsum('khq,kqn,kqhp->khnp', leave_w, write_part, input_part, precision=PRECISE)
    pulled = jnp.einsum('khq,kqn,kqhp->khnp', enter_w, read_part, grad_part, precision=PRECISE)
    return through, pushed, pulled


def piece_grads(input_part, write_part, read_part, grad_part, lower_mat, enter_w, leave_w, start_state, end_grad):
    span_len = lower_mat.shape[-1]
    pair_xy = jnp.einsum('kthp,kahp->khta', grad_part, input_part, precision=PRECISE)
    weighted = lower_mat * pair_xy
    cross_dot = jnp.einsum('ktn,kan->kta', read_part, write_part, precision=PRECISE)
    state_dy = jnp.einsum('khnp,kthp->kthn', start_state, grad_part, precision=PRECISE)
    grad_state = jnp.einsum('khnp,kthp->kthn', end_grad, input_part, precision=PRECISE)
    grad_c = jnp.einsum('khta,kan->ktn', weighted, write_part, precision=PRECISE)
    grad_c = grad_c + jnp.einsum('kht,kthn->ktn', enter_w, state_dy, precision=PRECISE)
    grad_b = jnp.einsum('khat,kan->ktn', weighted, read_part, precision=PRECISE)
    grad_b = grad_b + jnp.einsum('kht,kthn->ktn', leave_w, grad_state, precision=PRECISE)
    grad_x = jnp.einsum('khat,kahp->kthp', lower_mat * cross_dot[:, None], grad_part, precision=PRECISE)
    end_back = jnp.einsum('khnp,ktn->kthp', end_grad, write_part, precision=PRECISE)
    grad_x = grad_x + jnp.swapaxes(leave_w, 1, 2)[..., None] * end_back
    pair_terms = weighted * cross_dot[:, None]
    strict = jnp.arange(span_len)[None, :] < jnp.arange(span_len)[:, None]
    below_sum = lax.cumsum(pair_terms, axis=2, reverse=True)
    inner_sum = jnp.sum(jnp.where(strict, below_sum, 0.0), axis=-1)
    from_start = enter_w * jnp.einsum('ktn,kthn->kht', read_part, state_dy, precision=PRECISE)
    to_end = leave_w * jnp.einsum('ktn,kthn->kht', write_part, grad_state, precision=PRECISE)
    whole_term = enter_w[..., -1] * jnp.sum(end_grad * start_state, axis=(2, 3))
    later_sum = lax.cumsum(from_start, axis=2, reverse=True)
    earlier_sum = jnp.cumsum(to_end, axis=2) - to_end
    grad_l = inner_sum + later_sum + earlier_sum + whole_term[..., None]
    return grad_x, grad_b, grad_c, grad_l


def reference(queries, key_rows, value_rows, out_grad, ssm_input, state_write, state_read, log_decay, block_lists, rec_lengths):
    total_len = queries.shape[0]
    span = queries.shape[1]
    head_count = log_decay.shape[0]
    head_size = span // head_count
    block_count = block_lists.shape[0]
    block_len = total_len // block_count
    score_scale = head_size ** -0.5
    blocks_dev = TOK_DEV // BLOCK
    win_dev = KWIN // blocks_dev + 1
    win_blocks = win_dev * blocks_dev
    pad_blocks = win_blocks - blocks_dev
    device_count = block_count // blocks_dev
    positions = jnp.arange(total_len, dtype=jnp.int32)
    rec_ids = recording_of(positions, rec_lengths)
    keep_mask = keep_of(positions, rec_lengths)

    query_blocks = queries.astype(jnp.float32).reshape(block_count, block_len, head_count, head_size)
    key_blocks = key_rows.astype(jnp.float32).reshape(block_count, block_len, head_count, head_size)
    value_blocks = value_rows.astype(jnp.float32).reshape(block_count, block_len, head_count, head_size)
    grad_blocks = out_grad.astype(jnp.float32).reshape(block_count, block_len, head_count, head_size)

    def one_device(running, dev_id):
        grad_k_acc, grad_v_acc = running
        win_first = ((dev_id - win_dev + 1) * blocks_dev).astype(jnp.int32)

        def one_block(win_acc, local_id):
            win_k, win_v = win_acc
            block_id = (dev_id * blocks_dev + local_id).astype(jnp.int32)
            entries = block_lists[block_id]
            listed = entries >= 0
            key_ids = jnp.clip(entries, 0, block_count - 1).astype(jnp.int32)
            slot_ids = jnp.clip(entries - win_first, 0, win_blocks - 1).astype(jnp.int32)
            query_here = query_blocks[block_id]
            grad_here = grad_blocks[block_id]
            key_here = key_blocks[key_ids].reshape(-1, head_count, head_size)
            value_here = value_blocks[key_ids].reshape(-1, head_count, head_size)
            query_pos = block_id * block_len + jnp.arange(block_len, dtype=jnp.int32)
            key_pos = (entries[:, None] * block_len + jnp.arange(block_len, dtype=jnp.int32)[None, :]).reshape(-1)
            listed_cols = jnp.repeat(listed, block_len)
            allowed = listed_cols[None, :] & (recording_of(key_pos, rec_lengths)[None, :] == recording_of(query_pos, rec_lengths)[:, None]) & (key_pos[None, :] <= query_pos[:, None])
            scores = jnp.einsum('qhp,khp->hqk', query_here, key_here) * score_scale
            mask_b = allowed[None]
            exp_score = jnp.where(mask_b, jnp.exp(jnp.where(mask_b, scores, 0.0)), 0.0)
            denominator = jnp.sum(exp_score, axis=-1)
            weights = exp_score / denominator[..., None]
            grad_prob = jnp.einsum('qhp,khp->hqk', grad_here, value_here)
            row_delta = jnp.sum(weights * grad_prob, axis=-1)
            grad_score = lax.optimization_barrier((weights * (grad_prob - row_delta[..., None]) * score_scale).astype(jnp.bfloat16)).astype(jnp.float32)
            weights_b = lax.optimization_barrier(weights.astype(jnp.bfloat16)).astype(jnp.float32)
            grad_q = jnp.einsum('hqk,khp->qhp', grad_score, key_here)
            listed_f = listed.astype(grad_q.dtype)[:, None, None, None]
            part_k = jnp.einsum('hqk,qhp->khp', grad_score, query_here).reshape(-1, block_len, head_count, head_size) * listed_f
            part_v = jnp.einsum('hqk,qhp->khp', weights_b, grad_here).reshape(-1, block_len, head_count, head_size) * listed_f
            return (win_k.at[slot_ids].add(part_k), win_v.at[slot_ids].add(part_v)), grad_q

        win_zero = jnp.zeros((win_blocks, block_len, head_count, head_size), jnp.float32)
        (win_k, win_v), grad_q_dev = lax.scan(one_block, (win_zero, win_zero), jnp.arange(blocks_dev, dtype=jnp.int32))
        win_k, win_v = lax.optimization_barrier((win_k.astype(jnp.bfloat16), win_v.astype(jnp.bfloat16)))
        start = (dev_id * blocks_dev).astype(jnp.int32)
        grad_k_acc = lax.dynamic_update_slice_in_dim(grad_k_acc, lax.dynamic_slice_in_dim(grad_k_acc, start, win_blocks, 0) + win_k.astype(jnp.float32), start, 0)
        grad_v_acc = lax.dynamic_update_slice_in_dim(grad_v_acc, lax.dynamic_slice_in_dim(grad_v_acc, start, win_blocks, 0) + win_v.astype(jnp.float32), start, 0)
        return (grad_k_acc, grad_v_acc), grad_q_dev

    start_acc = jnp.zeros((block_count + pad_blocks, block_len, head_count, head_size), jnp.float32)
    (grad_k_acc, grad_v_acc), grad_q_all = lax.scan(one_device, (start_acc, start_acc), jnp.arange(device_count, dtype=jnp.int32))
    grad_queries = grad_q_all.reshape(total_len, span).astype(jnp.bfloat16)
    grad_keys = grad_k_acc[pad_blocks:].reshape(total_len, span).astype(jnp.bfloat16)
    grad_values = grad_v_acc[pad_blocks:].reshape(total_len, span).astype(jnp.bfloat16)

    piece_count = total_len // block_len
    pieces = (
        ssm_input.astype(jnp.float32).reshape(piece_count, 1, block_len, head_count, head_size),
        state_write.astype(jnp.float32).reshape(piece_count, 1, block_len, -1),
        state_read.astype(jnp.float32).reshape(piece_count, 1, block_len, -1),
        out_grad.astype(jnp.float32).reshape(piece_count, 1, block_len, head_count, head_size),
        jnp.transpose(log_decay.reshape(head_count, piece_count, block_len), (1, 0, 2))[:, None],
        keep_mask.reshape(piece_count, 1, block_len),
        rec_ids.reshape(piece_count, 1, block_len),
    )

    def summarize(element):
        lower_mat, enter_w, leave_w = piece_setup(element[4], element[5], element[6])
        return piece_summary(element[0], element[1], element[2], element[3], enter_w, leave_w)

    through, pushed, pulled = lax.map(summarize, pieces)
    through = through[:, 0]
    pushed = pushed[:, 0]
    pulled = pulled[:, 0]
    zero_state = jnp.zeros(pushed.shape[1:], pushed.dtype)

    def forward_step(running, element):
        return element[0][:, None, None] * running + element[1], running

    state_end, start_states = lax.scan(forward_step, zero_state, (through, pushed))

    def backward_step(running, element):
        return element[1] + element[0][:, None, None] * running, running

    grad_begin, end_grads = lax.scan(backward_step, zero_state, (through, pulled), reverse=True)

    def gradients(element):
        lower_mat, enter_w, leave_w = piece_setup(element[4], element[5], element[6])
        return piece_grads(element[0], element[1], element[2], element[3], lower_mat, enter_w, leave_w, element[7], element[8])

    grad_x, grad_b, grad_c, grad_l = lax.map(gradients, pieces + (start_states[:, None], end_grads[:, None]))
    grad_input = grad_x.reshape(total_len, span).astype(jnp.bfloat16)
    grad_write = grad_b.reshape(total_len, -1).astype(jnp.bfloat16)
    grad_read = grad_c.reshape(total_len, -1).astype(jnp.bfloat16)
    grad_decay = jnp.transpose(grad_l[:, 0], (1, 0, 2)).reshape(head_count, total_len)
    return grad_queries, grad_keys, grad_values, grad_input, grad_write, grad_read, grad_decay
```

```python
import functools

import jax
import jax.numpy as jnp
from jax import lax
from jax.experimental import pallas as pl
from jax.experimental.pallas import tpu as pltpu
from jax.sharding import PartitionSpec as P

KWIN = 4
F32 = jnp.float32
BF16 = jnp.bfloat16
HIGH = lax.Precision.HIGHEST


def dot(a, b, dims, precision=None):
    return lax.dot_general(a, b, (dims, ((), ())), precision=precision, preferred_element_type=F32)


NN = ((1,), (0,))
NT = ((1,), (1,))
TN = ((0,), (0,))


def mix_kernel(
    count,
    heads,
    q_ref,
    k_ref,
    v_ref,
    do_ref,
    x_ref,
    b_ref,
    c_ref,
    bias_ref,
    same_ref,
    cum_ref,
    cum_t_ref,
    gq_ref,
    gk_ref,
    gv_ref,
    gx_ref,
    gb_ref,
    gc_ref,
    gl_ref,
    kw,
    vw,
    pk,
    pv,
    rk,
    rv,
    wsum,
    send_sem,
    recv_sem,
    bsend_sem,
    brecv_sem,
):
    me = lax.axis_index("seq")
    rows, width = q_ref.shape
    size = width // heads
    scale = size ** (-0.5)
    own = KWIN * rows

    def place(dist):
        return pl.ds((KWIN - dist) * rows, rows)

    def forward(dist):
        return [
            pltpu.make_async_remote_copy(
                src_ref=src,
                dst_ref=dst.at[place(dist), :],
                send_sem=send_sem.at[dist - 1, i],
                recv_sem=recv_sem.at[dist - 1, i],
                device_id={"seq": me + dist},
                device_id_type=pl.DeviceIdType.MESH,
            )
            for i, (src, dst) in enumerate(((k_ref, kw), (v_ref, vw)))
        ]

    def backward(dist):
        return [
            pltpu.make_async_remote_copy(
                src_ref=src.at[place(dist), :],
                dst_ref=dst.at[dist - 1],
                send_sem=bsend_sem.at[dist - 1, i],
                recv_sem=brecv_sem.at[dist - 1, i],
                device_id={"seq": me - dist},
                device_id_type=pl.DeviceIdType.MESH,
            )
            for i, (src, dst) in enumerate(((pk, rk), (pv, rv)))
        ]

    barrier = pltpu.get_barrier_semaphore()
    for dist in range(1, KWIN + 1):

        @pl.when(me + dist < count)
        def _():
            pl.semaphore_signal(
                barrier, inc=1, device_id={"seq": me + dist}, device_id_type=pl.DeviceIdType.MESH
            )

        @pl.when(me - dist >= 0)
        def _():
            pl.semaphore_signal(
                barrier, inc=1, device_id={"seq": me - dist}, device_id_type=pl.DeviceIdType.MESH
            )

    peers = 0
    for dist in range(1, KWIN + 1):
        peers += (me + dist < count).astype(jnp.int32) + (me - dist >= 0).astype(jnp.int32)
    pl.semaphore_wait(barrier, peers)

    for dist in range(KWIN, 0, -1):

        @pl.when(me + dist < count)
        def _():
            for copy in forward(dist):
                copy.start()

    zero = jnp.zeros((rows, width), BF16)
    for dist in range(1, KWIN + 1):

        @pl.when(me - dist < 0)
        def _():
            kw[place(dist), :] = zero
            vw[place(dist), :] = zero

        @pl.when(me + dist >= count)
        def _():
            rk[dist - 1] = zero
            rv[dist - 1] = zero

    kw[pl.ds(own, rows), :] = k_ref[...]
    vw[pl.ds(own, rows), :] = v_ref[...]

    cross = dot(c_ref[...], b_ref[...], NT)
    row_id = lax.broadcasted_iota(jnp.int32, (rows, rows), 0)
    col_id = lax.broadcasted_iota(jnp.int32, (rows, rows), 1)
    upper = (col_id >= row_id).astype(BF16)
    strict = col_id < row_id
    lane = lax.broadcasted_iota(jnp.int32, (rows, gl_ref.shape[1]), 1)
    wsum[...] = jnp.zeros_like(wsum)
    gl = jnp.zeros(gl_ref.shape, F32)
    for first in range(0, heads, 2):
        cols = slice(first * size, (first + 2) * size)
        do2 = do_ref[:, cols]
        x2 = x_ref[:, cols]
        parts = []
        for i in range(2):
            h = first + i
            half = slice(i * size, (i + 1) * size)
            decay = jnp.exp(cum_t_ref[:, h : h + 1] - cum_ref[h : h + 1, :] + same_ref[...])
            pair = dot(do2[:, half], x2[:, half], NT)
            weighted = decay * pair
            wsum[...] += weighted
            mixed = decay * cross
            parts.append(dot(mixed.astype(BF16), do2[:, half], TN))
            terms = (weighted * cross).astype(BF16)
            below = dot(upper, terms, NN)
            inner = jnp.sum(jnp.where(strict, below, 0.0), axis=1, keepdims=True)
            gl = jnp.where(lane == h, inner, gl)
        gx_ref[:, cols] = jnp.concatenate(parts, axis=1)
    gl_ref[...] = gl
    weighted = wsum[...].astype(BF16)
    gc_ref[...] = dot(weighted, b_ref[...], NN)
    gb_ref[...] = dot(weighted, c_ref[...], TN)

    for dist in range(1, KWIN + 1):

        @pl.when(me - dist >= 0)
        def _():
            for copy in forward(dist):
                copy.wait_recv()

    def pair_of_heads(step, carry):
        cols = pl.ds(pl.multiple_of(step * 2 * size, 2 * size), 2 * size)
        q2, do2 = q_ref[:, cols], do_ref[:, cols]
        k2, v2 = kw[:, cols], vw[:, cols]
        gq, gk, gv = [], [], []
        for i in range(2):
            half = slice(i * size, (i + 1) * size)
            qh, kh, vh, dh = q2[:, half], k2[:, half], v2[:, half], do2[:, half]
            e = jnp.exp(dot(qh, kh, NT) * scale + bias_ref[...])
            prob = e * (1.0 / jnp.sum(e, axis=1, keepdims=True))
            dprob = dot(dh, vh, NT)
            delta = jnp.sum(prob * dprob, axis=1, keepdims=True)
            ds = (prob * (dprob - delta) * scale).astype(BF16)
            gq.append(dot(ds, kh, NN))
            gk.append(dot(ds, qh, TN))
            gv.append(dot(prob.astype(BF16), dh, TN))
        gq_ref[:, cols] = jnp.concatenate(gq, axis=1).astype(BF16)
        pk[:, cols] = jnp.concatenate(gk, axis=1).astype(BF16)
        pv[:, cols] = jnp.concatenate(gv, axis=1).astype(BF16)
        return carry

    lax.fori_loop(0, heads // 2, pair_of_heads, 0)

    for dist in range(KWIN, 0, -1):

        @pl.when(me - dist >= 0)
        def _():
            for copy in backward(dist):
                copy.start()

    for dist in range(1, KWIN + 1):

        @pl.when(me + dist < count)
        def _():
            for copy in forward(dist):
                copy.wait_send()
            for copy in backward(dist):
                copy.wait_recv()

    total_k = pk[pl.ds(own, rows), :].astype(F32)
    total_v = pv[pl.ds(own, rows), :].astype(F32)
    for dist in range(1, KWIN + 1):
        total_k = total_k + rk[dist - 1].astype(F32)
        total_v = total_v + rv[dist - 1].astype(F32)
    gk_ref[...] = total_k.astype(BF16)
    gv_ref[...] = total_v.astype(BF16)

    for dist in range(1, KWIN + 1):

        @pl.when(me - dist >= 0)
        def _():
            for copy in backward(dist):
                copy.wait_send()


def join_kernel(
    heads,
    state_ref,
    grad_ref,
    xl_ref,
    de_ref,
    leave_ref,
    b_ref,
    c_ref,
    through_ref,
    gxi_ref,
    gbi_ref,
    gci_ref,
    gli_ref,
    gx_ref,
    gb_ref,
    gc_ref,
    gl_ref,
):
    rows, width = gx_ref.shape
    size = width // heads
    lanes = gl_ref.shape[1]
    state, grad = state_ref[...], grad_ref[...]
    state_b, grad_b = state.astype(BF16), grad.astype(BF16)
    xl, de = xl_ref[...], de_ref[...]
    gc_ref[...] = (gci_ref[...] + dot(de, state_b, NN)).astype(BF16)
    gb_ref[...] = (gbi_ref[...] + dot(xl, grad_b, NN)).astype(BF16)
    back = dot(b_ref[...], grad_b, NT)
    ahead = dot(c_ref[...], state_b, NT)
    gx_ref[...] = (gxi_ref[...] + leave_ref[...].astype(F32) * back).astype(BF16)
    owner = lax.broadcasted_iota(jnp.int32, (width, lanes), 0) // size
    pick = (owner == lax.broadcasted_iota(jnp.int32, (width, lanes), 1)).astype(F32)
    from_start = dot(de.astype(F32) * ahead, pick, NN, HIGH)
    to_end = dot(xl.astype(F32) * back, pick, NN, HIGH)
    row_id = lax.broadcasted_iota(jnp.int32, (rows, rows), 0)
    col_id = lax.broadcasted_iota(jnp.int32, (rows, rows), 1)
    later = dot((col_id >= row_id).astype(F32), from_start, NN, HIGH)
    earlier = dot((col_id < row_id).astype(F32), to_end, NN, HIGH)
    each = dot(jnp.ones((8, state.shape[1]), F32), grad * state, NT, HIGH)
    whole = dot(each, pick, NN, HIGH)[:1] * through_ref[...]
    gl_ref[...] = gli_ref[...] + later + earlier + whole


def body(
    queries,
    key_rows,
    value_rows,
    out_grad,
    ssm_input,
    state_write,
    state_read,
    log_decay,
    block_lists,
    rec_lengths,
):
    rows, width = queries.shape
    heads = log_decay.shape[0]
    size = width // heads
    states = state_write.shape[1]
    lanes = 128
    count = lax.axis_size("seq")
    me = lax.axis_index("seq")
    assert block_lists.shape[0] == 1

    ends = jnp.sum(
        jnp.where(
            jnp.arange(rec_lengths.shape[0])[:, None] >= jnp.arange(rec_lengths.shape[0])[None, :],
            rec_lengths[None, :],
            0,
        ),
        axis=1,
    )
    window = (me - KWIN) * rows + jnp.arange((KWIN + 1) * rows, dtype=jnp.int32)
    rec = jnp.sum((window[:, None] >= ends[None, :]).astype(jnp.int32), axis=1)
    own_pos, own_rec = window[KWIN * rows :], rec[KWIN * rows :]
    listed = jnp.any(block_lists[0][None, :] == (window // rows)[:, None], axis=1) & (window >= 0)
    allowed = (
        listed[None, :]
        & (rec[None, :] == own_rec[:, None])
        & (window[None, :] <= own_pos[:, None])
    )
    bias = jnp.where(allowed, 0.0, -1e30).astype(F32)
    same = jnp.where(
        (own_pos[:, None] >= own_pos[None, :]) & (own_rec[:, None] == own_rec[None, :]), 0.0, -1e30
    ).astype(F32)

    tri = (jnp.arange(rows)[:, None] <= jnp.arange(rows)[None, :]).astype(F32)
    cum = jnp.dot(log_decay, tri, precision=HIGH)
    first_keep = jnp.where(jnp.any(ends == own_pos[0]) | (own_pos[0] == 0), 0.0, 1.0)
    enter = jnp.exp(cum) * (first_keep * (own_rec == own_rec[0]).astype(F32))
    leave = jnp.exp(cum[:, -1:] - cum) * (own_rec == own_rec[-1]).astype(F32)
    through = enter[:, -1]
    leave_wide = jnp.repeat(leave.T, size, axis=1)
    enter_wide = jnp.repeat(enter.T, size, axis=1)
    xl = (ssm_input.astype(F32) * leave_wide).astype(BF16)
    de = (out_grad.astype(F32) * enter_wide).astype(BF16)
    pushed = dot(xl, state_write, TN).astype(BF16)
    pulled = dot(de, state_read, TN).astype(BF16)
    coarse = lax.reduce_precision(through, 8, 7)
    fine = lax.reduce_precision(through - coarse, 8, 7)
    tail = jnp.zeros((16, states), F32).at[0, :heads].set(coarse).at[1, :heads].set(fine)
    packed = jnp.concatenate([pushed, pulled, tail.astype(BF16)], axis=0)
    gathered = lax.all_gather(packed, "seq")

    vmem = pl.BlockSpec(memory_space=pltpu.VMEM)
    wide = jax.ShapeDtypeStruct((rows, width), BF16)
    gq, gk, gv, gxi, gbi, gci, gli = pl.pallas_call(
        functools.partial(mix_kernel, count, heads),
        out_shape=(
            wide,
            wide,
            wide,
            jax.ShapeDtypeStruct((rows, width), F32),
            jax.ShapeDtypeStruct((rows, states), F32),
            jax.ShapeDtypeStruct((rows, states), F32),
            jax.ShapeDtypeStruct((rows, lanes), F32),
        ),
        in_specs=[vmem] * 11,
        out_specs=(vmem,) * 7,
        scratch_shapes=[pltpu.VMEM(((KWIN + 1) * rows, width), BF16)] * 4
        + [pltpu.VMEM((KWIN, rows, width), BF16)] * 2
        + [pltpu.VMEM((rows, rows), F32)]
        + [pltpu.SemaphoreType.DMA((KWIN, 2))] * 4,
        compiler_params=pltpu.CompilerParams(
            collective_id=0, has_side_effects=True, vmem_limit_bytes=40 * 2**20
        ),
        cost_estimate=pl.CostEstimate(
            flops=10**10, bytes_accessed=3 * 10**7, transcendentals=10**6
        ),
    )(
        queries,
        key_rows,
        value_rows,
        out_grad,
        ssm_input,
        state_write,
        state_read,
        bias,
        same,
        cum,
        cum.T,
    )

    each = gathered[:, 2 * width, :heads].astype(F32) + gathered[:, 2 * width + 1, :heads].astype(
        F32
    )
    ids = jnp.arange(count)
    src, mid = ids[:, None], ids[None, :]
    between_f = (mid > src) & (mid < me)
    between_b = (mid < src) & (mid > me)
    weight_f = jnp.prod(jnp.where(between_f[:, :, None], each[None], 1.0), axis=1)
    weight_b = jnp.prod(jnp.where(between_b[:, :, None], each[None], 1.0), axis=1)
    weight_f = jnp.where((ids < me)[:, None], weight_f, 0.0)
    weight_b = jnp.where((ids > me)[:, None], weight_b, 0.0)
    parts = gathered[:, : 2 * width].reshape(count, 2, heads, size, states).astype(F32)
    weights = jnp.stack([weight_f, weight_b], axis=1)[..., None, None]
    joined = jnp.sum(parts * weights, axis=0).reshape(2, width, states)

    grad_input, grad_write, grad_read, grad_l = pl.pallas_call(
        functools.partial(join_kernel, heads),
        out_shape=(
            wide,
            jax.ShapeDtypeStruct((rows, states), BF16),
            jax.ShapeDtypeStruct((rows, states), BF16),
            jax.ShapeDtypeStruct((rows, lanes), F32),
        ),
        in_specs=[vmem] * 12,
        out_specs=(vmem,) * 4,
        compiler_params=pltpu.CompilerParams(vmem_limit_bytes=40 * 2**20),
    )(
        joined[0],
        joined[1],
        xl,
        de,
        leave_wide,
        state_write,
        state_read,
        jnp.pad(through, (0, lanes - heads))[None],
        gxi,
        gbi,
        gci,
        gli,
    )
    return (gq, gk, gv, grad_input, grad_write, grad_read, grad_l[:, :heads].T)


def solution(mesh):
    rows = P(("grp", "seq"), None)
    turned = P(None, ("grp", "seq"))
    return jax.shard_map(
        body,
        mesh=mesh,
        in_specs=(rows,) * 7 + (turned, rows, P("grp")),
        out_specs=(rows,) * 6 + (turned,),
        check_vma=False,
    )
```

```python
import functools

import jax
import jax.numpy as jnp
from jax import lax
from jax.experimental import pallas as pl
from jax.experimental.pallas import tpu as pltpu
from jax.sharding import PartitionSpec as P

KWIN = 4
PARTS = 2
F32 = jnp.float32
BF16 = jnp.bfloat16
HIGH = lax.Precision.HIGHEST


def dot(a, b, dims, precision=None):
    return lax.dot_general(a, b, (dims, ((), ())), precision=precision, preferred_element_type=F32)


NN = ((1,), (0,))
NT = ((1,), (1,))
TN = ((0,), (0,))


def mix_kernel(
    count,
    heads,
    q_ref,
    k_ref,
    v_ref,
    do_ref,
    x_ref,
    b_ref,
    c_ref,
    bias_ref,
    same_ref,
    cum_ref,
    cum_t_ref,
    gq_ref,
    gk_ref,
    gv_ref,
    gx_ref,
    gb_ref,
    gc_ref,
    gl_ref,
    kw,
    vw,
    pk,
    pv,
    rk,
    rv,
    wsum,
    total,
    send_sem,
    recv_sem,
    bsend_sem,
    brecv_sem,
):
    me = lax.axis_index("seq")
    rows, width = q_ref.shape
    size = width // heads
    scale = size ** (-0.5)
    odd = lax.rem(me, 2)
    side = lax.div(lax.rem(me, KWIN), 2)
    mate = me + 1 - 2 * odd
    across = me + 2 - 4 * side
    part = width // PARTS

    def place(slot):
        return pl.ds(pl.multiple_of((KWIN - slot) * rows, rows), rows)

    routes = (
        (0, KWIN, me + KWIN),
        (KWIN * side, 2, across),
        (KWIN * odd, 1 + 2 * odd, mate),
        (2, 3 - 2 * odd, mate),
    )

    def forward(hop, i):
        src, dst, device = routes[hop]
        ref = (kw, vw)[i]
        return pltpu.make_async_remote_copy(
            src_ref=ref.at[place(src), :],
            dst_ref=ref.at[place(dst), :],
            send_sem=send_sem.at[hop, i],
            recv_sem=recv_sem.at[hop, i],
            device_id={"seq": device},
            device_id_type=pl.DeviceIdType.MESH,
        )

    backs = ((KWIN, me - KWIN), (2, across), (3 - 2 * odd, mate), (1 + 2 * odd, mate))

    def backward(hop, i, c):
        src, device = backs[hop]
        cols = pl.ds(c * part, part)
        return pltpu.make_async_remote_copy(
            src_ref=(pk, pv)[i].at[place(src), cols],
            dst_ref=(rk, rv)[i].at[hop, :, cols],
            send_sem=bsend_sem.at[hop, i * PARTS + c],
            recv_sem=brecv_sem.at[hop, i * PARTS + c],
            device_id={"seq": device},
            device_id_type=pl.DeviceIdType.MESH,
        )

    barrier = pltpu.get_barrier_semaphore()
    for device in (mate, across):
        pl.semaphore_signal(
            barrier, inc=1, device_id={"seq": device}, device_id_type=pl.DeviceIdType.MESH
        )

    @pl.when(me + KWIN < count)
    def _():
        pl.semaphore_signal(
            barrier, inc=1, device_id={"seq": me + KWIN}, device_id_type=pl.DeviceIdType.MESH
        )

    @pl.when(me - KWIN >= 0)
    def _():
        pl.semaphore_signal(
            barrier, inc=1, device_id={"seq": me - KWIN}, device_id_type=pl.DeviceIdType.MESH
        )

    kw[place(0), :] = k_ref[...]
    vw[place(0), :] = v_ref[...]

    @pl.when(me < KWIN)
    def _():
        kw[place(KWIN), :] = jnp.zeros((rows, width), BF16)
        vw[place(KWIN), :] = jnp.zeros((rows, width), BF16)

    peers = 2 + (me + KWIN < count).astype(jnp.int32) + (me - KWIN >= 0).astype(jnp.int32)
    pl.semaphore_wait(barrier, peers)

    for i in range(2):

        @pl.when(me + KWIN < count)
        def _():
            forward(0, i).start()

        @pl.when(side == 0)
        def _():
            forward(1, i).start()

        @pl.when(odd == 0)
        def _():
            forward(2, i).start()

    cross = dot(c_ref[...], b_ref[...], NT)
    row_id = lax.broadcasted_iota(jnp.int32, (rows, rows), 0)
    col_id = lax.broadcasted_iota(jnp.int32, (rows, rows), 1)
    upper = (col_id >= row_id).astype(BF16)
    strict = col_id < row_id
    lane = lax.broadcasted_iota(jnp.int32, (rows, gl_ref.shape[1]), 1)
    wsum[...] = jnp.zeros_like(wsum)
    gl = jnp.zeros(gl_ref.shape, F32)
    for first in range(0, heads, 2):
        cols = slice(first * size, (first + 2) * size)
        do2 = do_ref[:, cols]
        x2 = x_ref[:, cols]
        parts = []
        for i in range(2):
            h = first + i
            half = slice(i * size, (i + 1) * size)
            decay = jnp.exp(cum_t_ref[:, h : h + 1] - cum_ref[h : h + 1, :] + same_ref[...])
            pair = dot(do2[:, half], x2[:, half], NT)
            weighted = decay * pair
            wsum[...] += weighted
            mixed = decay * cross
            parts.append(dot(mixed.astype(BF16), do2[:, half], TN))
            terms = (weighted * cross).astype(BF16)
            below = dot(upper, terms, NN)
            inner = jnp.sum(jnp.where(strict, below, 0.0), axis=1, keepdims=True)
            gl = jnp.where(lane == h, inner, gl)
        gx_ref[:, cols] = jnp.concatenate(parts, axis=1)
    gl_ref[...] = gl
    weighted = wsum[...].astype(BF16)
    gc_ref[...] = dot(weighted, b_ref[...], NN)
    gb_ref[...] = dot(weighted, c_ref[...], TN)

    for i in range(2):

        @pl.when(me - KWIN >= 0)
        def _():
            forward(0, i).wait_recv()

        @pl.when(side == 1)
        def _():
            forward(1, i).start()

        @pl.when(odd == 1)
        def _():
            forward(2, i).start()

    for i in range(2):
        forward(1, i).wait_recv()
        forward(3, i).start()
    for i in range(2):
        forward(2, i).wait_recv()
        forward(3, i).wait_recv()

    def pair_of_heads(step, carry):
        cols = pl.ds(pl.multiple_of(step * 2 * size, 2 * size), 2 * size)
        q2, do2 = q_ref[:, cols], do_ref[:, cols]
        k2, v2 = kw[:, cols], vw[:, cols]
        gq, gk, gv = [], [], []
        for i in range(2):
            half = slice(i * size, (i + 1) * size)
            qh, kh, vh, dh = q2[:, half], k2[:, half], v2[:, half], do2[:, half]
            e = jnp.exp(dot(qh, kh, NT) * scale + bias_ref[...])
            prob = e * (1.0 / jnp.sum(e, axis=1, keepdims=True))
            dprob = dot(dh, vh, NT)
            delta = jnp.sum(prob * dprob, axis=1, keepdims=True)
            ds = (prob * (dprob - delta) * scale).astype(BF16)
            gq.append(dot(ds, kh, NN))
            gk.append(dot(ds, qh, TN))
            gv.append(dot(prob.astype(BF16), dh, TN))
        gq_ref[:, cols] = jnp.concatenate(gq, axis=1).astype(BF16)
        pk[:, cols] = jnp.concatenate(gk, axis=1).astype(BF16)
        pv[:, cols] = jnp.concatenate(gv, axis=1).astype(BF16)
        return carry

    def add(i, c, slot, hop):
        cols = pl.ds(c * part, part)
        ref, got = (pk, pv)[i], (rk, rv)[i]
        ref[place(slot), cols] = (
            ref[place(slot), cols].astype(F32) + got[hop, :, cols].astype(F32)
        ).astype(BF16)

    def pass_across(c):
        for i in range(2):
            backward(3, i, c).wait_recv()
            add(i, c, 2, 3)
            backward(1, i, c).start()

    def pass_back(c):
        for i in range(2):
            backward(2, i, c).wait_recv()
            backward(1, i, c).wait_recv()
            cols = pl.ds(c * part, part)
            ref, got = (pk, pv)[i], (rk, rv)[i]
            near = got[2, :, cols].astype(F32)
            far = got[1, :, cols].astype(F32)
            near_own = (1 - odd).astype(F32)
            far_own = (1 - side).astype(F32)
            through = near * (1.0 - near_own) + far * (1.0 - far_own)
            kept = near * near_own + far * far_own
            ref[place(KWIN), cols] = (
                ref[place(KWIN), cols].astype(F32) + through
            ).astype(BF16)

            @pl.when(me - KWIN >= 0)
            def _():
                backward(0, i, c).start()

            total[i, :, cols] = ref[place(0), cols].astype(F32) + kept

    pairs = heads // 2 // PARTS
    for c in range(PARTS):
        lax.fori_loop(c * pairs, (c + 1) * pairs, pair_of_heads, 0)
        for hop in (3, 2):
            for i in range(2):
                backward(hop, i, c).start()
        if c > 0:
            pass_across(c - 1)
    pass_across(PARTS - 1)
    for c in range(PARTS):
        pass_back(c)

    for i in range(2):

        @pl.when(me + KWIN < count)
        def _():
            forward(0, i).wait_send()
            for c in range(PARTS):
                cols = pl.ds(c * part, part)
                backward(0, i, c).wait_recv()
                total[i, :, cols] = total[i, :, cols] + (rk, rv)[i][0, :, cols].astype(F32)

        for hop in range(1, KWIN):
            forward(hop, i).wait_send()
            for c in range(PARTS):
                backward(hop, i, c).wait_send()

        @pl.when(me - KWIN >= 0)
        def _():
            for c in range(PARTS):
                backward(0, i, c).wait_send()

    gk_ref[...] = total[0].astype(BF16)
    gv_ref[...] = total[1].astype(BF16)


def join_kernel(
    heads,
    state_ref,
    grad_ref,
    xl_ref,
    de_ref,
    leave_ref,
    b_ref,
    c_ref,
    through_ref,
    gxi_ref,
    gbi_ref,
    gci_ref,
    gli_ref,
    gx_ref,
    gb_ref,
    gc_ref,
    gl_ref,
):
    rows, width = gx_ref.shape
    size = width // heads
    lanes = gl_ref.shape[1]
    state, grad = state_ref[...], grad_ref[...]
    state_b, grad_b = state.astype(BF16), grad.astype(BF16)
    xl, de = xl_ref[...], de_ref[...]
    gc_ref[...] = (gci_ref[...] + dot(de, state_b, NN)).astype(BF16)
    gb_ref[...] = (gbi_ref[...] + dot(xl, grad_b, NN)).astype(BF16)
    back = dot(b_ref[...], grad_b, NT)
    ahead = dot(c_ref[...], state_b, NT)
    gx_ref[...] = (gxi_ref[...] + leave_ref[...].astype(F32) * back).astype(BF16)
    owner = lax.broadcasted_iota(jnp.int32, (width, lanes), 0) // size
    pick = (owner == lax.broadcasted_iota(jnp.int32, (width, lanes), 1)).astype(F32)
    from_start = dot(de.astype(F32) * ahead, pick, NN, HIGH)
    to_end = dot(xl.astype(F32) * back, pick, NN, HIGH)
    row_id = lax.broadcasted_iota(jnp.int32, (rows, rows), 0)
    col_id = lax.broadcasted_iota(jnp.int32, (rows, rows), 1)
    later = dot((col_id >= row_id).astype(F32), from_start, NN, HIGH)
    earlier = dot((col_id < row_id).astype(F32), to_end, NN, HIGH)
    each = dot(jnp.ones((8, state.shape[1]), F32), grad * state, NT, HIGH)
    whole = dot(each, pick, NN, HIGH)[:1] * through_ref[...]
    gl_ref[...] = gli_ref[...] + later + earlier + whole


def body(
    queries,
    key_rows,
    value_rows,
    out_grad,
    ssm_input,
    state_write,
    state_read,
    log_decay,
    block_lists,
    rec_lengths,
):
    rows, width = queries.shape
    heads = log_decay.shape[0]
    size = width // heads
    states = state_write.shape[1]
    lanes = 128
    count = lax.axis_size("seq")
    me = lax.axis_index("seq")
    assert block_lists.shape[0] == 1

    ends = jnp.sum(
        jnp.where(
            jnp.arange(rec_lengths.shape[0])[:, None] >= jnp.arange(rec_lengths.shape[0])[None, :],
            rec_lengths[None, :],
            0,
        ),
        axis=1,
    )
    window = (me - KWIN) * rows + jnp.arange((KWIN + 1) * rows, dtype=jnp.int32)
    rec = jnp.sum((window[:, None] >= ends[None, :]).astype(jnp.int32), axis=1)
    own_pos, own_rec = window[KWIN * rows :], rec[KWIN * rows :]
    listed = jnp.any(block_lists[0][None, :] == (window // rows)[:, None], axis=1) & (window >= 0)
    allowed = (
        listed[None, :]
        & (rec[None, :] == own_rec[:, None])
        & (window[None, :] <= own_pos[:, None])
    )
    bias = jnp.where(allowed, 0.0, -1e30).astype(F32)
    same = jnp.where(
        (own_pos[:, None] >= own_pos[None, :]) & (own_rec[:, None] == own_rec[None, :]), 0.0, -1e30
    ).astype(F32)

    tri = (jnp.arange(rows)[:, None] <= jnp.arange(rows)[None, :]).astype(F32)
    cum = jnp.dot(log_decay, tri, precision=HIGH)
    first_keep = jnp.where(jnp.any(ends == own_pos[0]) | (own_pos[0] == 0), 0.0, 1.0)
    enter = jnp.exp(cum) * (first_keep * (own_rec == own_rec[0]).astype(F32))
    leave = jnp.exp(cum[:, -1:] - cum) * (own_rec == own_rec[-1]).astype(F32)
    through = enter[:, -1]
    leave_wide = jnp.repeat(leave.T, size, axis=1)
    enter_wide = jnp.repeat(enter.T, size, axis=1)
    xl = (ssm_input.astype(F32) * leave_wide).astype(BF16)
    de = (out_grad.astype(F32) * enter_wide).astype(BF16)
    pushed = dot(xl, state_write, TN).astype(BF16)
    pulled = dot(de, state_read, TN).astype(BF16)
    coarse = lax.reduce_precision(through, 8, 7)
    fine = lax.reduce_precision(through - coarse, 8, 7)
    tail = jnp.zeros((16, states), F32).at[0, :heads].set(coarse).at[1, :heads].set(fine)
    packed = jnp.concatenate([pushed, pulled, tail.astype(BF16)], axis=0)
    gathered = lax.all_gather(packed, "seq")

    vmem = pl.BlockSpec(memory_space=pltpu.VMEM)
    wide = jax.ShapeDtypeStruct((rows, width), BF16)
    gq, gk, gv, gxi, gbi, gci, gli = pl.pallas_call(
        functools.partial(mix_kernel, count, heads),
        out_shape=(
            wide,
            wide,
            wide,
            jax.ShapeDtypeStruct((rows, width), F32),
            jax.ShapeDtypeStruct((rows, states), F32),
            jax.ShapeDtypeStruct((rows, states), F32),
            jax.ShapeDtypeStruct((rows, lanes), F32),
        ),
        in_specs=[vmem] * 11,
        out_specs=(vmem,) * 7,
        scratch_shapes=[pltpu.VMEM(((KWIN + 1) * rows, width), BF16)] * 4
        + [pltpu.VMEM((KWIN, rows, width), BF16)] * 2
        + [pltpu.VMEM((rows, rows), F32), pltpu.VMEM((2, rows, width), F32)]
        + [pltpu.SemaphoreType.DMA((KWIN, 2))] * 2
        + [pltpu.SemaphoreType.DMA((KWIN, 2 * PARTS))] * 2,
        compiler_params=pltpu.CompilerParams(
            collective_id=0, has_side_effects=True, vmem_limit_bytes=40 * 2**20
        ),
        cost_estimate=pl.CostEstimate(
            flops=10**10, bytes_accessed=3 * 10**7, transcendentals=10**6
        ),
    )(
        queries,
        key_rows,
        value_rows,
        out_grad,
        ssm_input,
        state_write,
        state_read,
        bias,
        same,
        cum,
        cum.T,
    )

    each = gathered[:, 2 * width, :heads].astype(F32) + gathered[:, 2 * width + 1, :heads].astype(
        F32
    )
    ids = jnp.arange(count)
    src, mid = ids[:, None], ids[None, :]
    between_f = (mid > src) & (mid < me)
    between_b = (mid < src) & (mid > me)
    weight_f = jnp.prod(jnp.where(between_f[:, :, None], each[None], 1.0), axis=1)
    weight_b = jnp.prod(jnp.where(between_b[:, :, None], each[None], 1.0), axis=1)
    weight_f = jnp.where((ids < me)[:, None], weight_f, 0.0)
    weight_b = jnp.where((ids > me)[:, None], weight_b, 0.0)
    parts = gathered[:, : 2 * width].reshape(count, 2, heads, size, states).astype(F32)
    weights = jnp.stack([weight_f, weight_b], axis=1)[..., None, None]
    joined = jnp.sum(parts * weights, axis=0).reshape(2, width, states)

    grad_input, grad_write, grad_read, grad_l = pl.pallas_call(
        functools.partial(join_kernel, heads),
        out_shape=(
            wide,
            jax.ShapeDtypeStruct((rows, states), BF16),
            jax.ShapeDtypeStruct((rows, states), BF16),
            jax.ShapeDtypeStruct((rows, lanes), F32),
        ),
        in_specs=[vmem] * 12,
        out_specs=(vmem,) * 4,
        compiler_params=pltpu.CompilerParams(vmem_limit_bytes=40 * 2**20),
    )(
        joined[0],
        joined[1],
        xl,
        de,
        leave_wide,
        state_write,
        state_read,
        jnp.pad(through, (0, lanes - heads))[None],
        gxi,
        gbi,
        gci,
        gli,
    )
    return (gq, gk, gv, grad_input, grad_write, grad_read, grad_l[:, :heads].T)


def solution(mesh):
    rows = P(("grp", "seq"), None)
    turned = P(None, ("grp", "seq"))
    return jax.shard_map(
        body,
        mesh=mesh,
        in_specs=(rows,) * 7 + (turned, rows, P("grp")),
        out_specs=(rows,) * 6 + (turned,),
        check_vma=False,
    )
```

```python
import functools

import jax
import jax.numpy as jnp
from jax import lax
from jax.experimental import pallas as pl
from jax.experimental.pallas import tpu as pltpu
from jax.sharding import PartitionSpec as P

KWIN = 4
PARTS = 2
F32 = jnp.float32
BF16 = jnp.bfloat16
HIGH = lax.Precision.HIGHEST


def dot(a, b, dims, precision=None):
    return lax.dot_general(a, b, (dims, ((), ())), precision=precision, preferred_element_type=F32)


NN = ((1,), (0,))
NT = ((1,), (1,))
TN = ((0,), (0,))


def mix_kernel(
    count,
    heads,
    q_ref,
    k_ref,
    v_ref,
    do_ref,
    x_ref,
    b_ref,
    c_ref,
    bias_ref,
    same_ref,
    cum_ref,
    cum_t_ref,
    u_ref,
    a_ref,
    gq_ref,
    gk_ref,
    gv_ref,
    gx_ref,
    gb_ref,
    gc_ref,
    gl_ref,
    st_ref,
    kw,
    vw,
    pk,
    pv,
    rk,
    rv,
    wsum,
    total,
    got_u,
    got,
    got_a,
    duo,
    pair_a,
    chain,
    chain_in,
    plane_sum,
    plane_a,
    ssend_sem,
    srecv_sem,
    send_sem,
    recv_sem,
    bsend_sem,
    brecv_sem,
):
    me = lax.axis_index("seq")
    rows, width = q_ref.shape
    size = width // heads
    scale = size ** (-0.5)
    odd = lax.rem(me, 2)
    side = lax.div(lax.rem(me, KWIN), 2)
    mate = me + 1 - 2 * odd
    across = me + 2 - 4 * side
    part = width // PARTS

    def place(slot):
        return pl.ds(pl.multiple_of((KWIN - slot) * rows, rows), rows)

    routes = (
        (0, KWIN, me + KWIN),
        (KWIN * side, 2, across),
        (KWIN * odd, 1 + 2 * odd, mate),
        (2, 3 - 2 * odd, mate),
    )

    def forward(hop, i):
        src, dst, device = routes[hop]
        ref = (kw, vw)[i]
        return pltpu.make_async_remote_copy(
            src_ref=ref.at[place(src), :],
            dst_ref=ref.at[place(dst), :],
            send_sem=send_sem.at[hop, i],
            recv_sem=recv_sem.at[hop, i],
            device_id={"seq": device},
            device_id_type=pl.DeviceIdType.MESH,
        )

    backs = ((KWIN, me - KWIN), (2, across), (3 - 2 * odd, mate), (1 + 2 * odd, mate))

    def backward(hop, i, c):
        src, device = backs[hop]
        cols = pl.ds(c * part, part)
        return pltpu.make_async_remote_copy(
            src_ref=(pk, pv)[i].at[place(src), cols],
            dst_ref=(rk, rv)[i].at[hop, :, cols],
            send_sem=bsend_sem.at[hop, i * PARTS + c],
            recv_sem=brecv_sem.at[hop, i * PARTS + c],
            device_id={"seq": device},
            device_id_type=pl.DeviceIdType.MESH,
        )

    def state_copy(src, dst, device, level, i):
        return pltpu.make_async_remote_copy(
            src_ref=src,
            dst_ref=dst,
            send_sem=ssend_sem.at[level, i],
            recv_sem=srecv_sem.at[level, i],
            device_id={"seq": device},
            device_id_type=pl.DeviceIdType.MESH,
        )

    def exchange(level):
        src, src_a, device = ((u_ref, a_ref, mate), (duo, pair_a, across))[level]
        return (
            state_copy(src, (got_u, got)[level], device, level, 0),
            state_copy(src_a, got_a.at[level], device, level, 1),
        )

    def chain_copy(i):
        return state_copy(chain.at[i], chain_in.at[i], me + (KWIN, -KWIN)[i], 2, i)

    last = lax.div(count - 1, KWIN)
    plane = lax.div(me, KWIN)
    away = (plane, last - plane)

    def chain_step(i, now):
        @pl.when(now)
        def _():
            @pl.when(away[i] > 0)
            def _():
                chain_copy(i).wait_recv()

            @pl.when(away[1 - i] > 0)
            def _():
                chain[i] = (
                    plane_sum[i] + plane_a[0, :1, :] * chain_in[i]
                )
                chain_copy(i).start()

    barrier = pltpu.get_barrier_semaphore()
    for device in (mate, across):
        pl.semaphore_signal(
            barrier, inc=1, device_id={"seq": device}, device_id_type=pl.DeviceIdType.MESH
        )

    @pl.when(me + KWIN < count)
    def _():
        pl.semaphore_signal(
            barrier, inc=1, device_id={"seq": me + KWIN}, device_id_type=pl.DeviceIdType.MESH
        )

    @pl.when(me - KWIN >= 0)
    def _():
        pl.semaphore_signal(
            barrier, inc=1, device_id={"seq": me - KWIN}, device_id_type=pl.DeviceIdType.MESH
        )

    kw[place(0), :] = k_ref[...]
    vw[place(0), :] = v_ref[...]

    @pl.when(me < KWIN)
    def _():
        kw[place(KWIN), :] = jnp.zeros((rows, width), BF16)
        vw[place(KWIN), :] = jnp.zeros((rows, width), BF16)

    peers = 2 + (me + KWIN < count).astype(jnp.int32) + (me - KWIN >= 0).astype(jnp.int32)
    pl.semaphore_wait(barrier, peers)

    for copy in exchange(0):
        copy.start()

    for i in range(2):

        @pl.when(away[i] == 0)
        def _():
            chain_in[i] = jnp.zeros(chain_in.shape[1:], F32)

    for i in range(2):

        @pl.when(me + KWIN < count)
        def _():
            forward(0, i).start()

        @pl.when(side == 0)
        def _():
            forward(1, i).start()

        @pl.when(odd == 0)
        def _():
            forward(2, i).start()

    cross = dot(c_ref[...], b_ref[...], NT)
    row_id = lax.broadcasted_iota(jnp.int32, (rows, rows), 0)
    col_id = lax.broadcasted_iota(jnp.int32, (rows, rows), 1)
    upper = (col_id >= row_id).astype(BF16)
    strict = col_id < row_id
    lane = lax.broadcasted_iota(jnp.int32, (rows, gl_ref.shape[1]), 1)
    wsum[...] = jnp.zeros_like(wsum)
    gl = jnp.zeros(gl_ref.shape, F32)
    for first in range(0, heads, 2):
        cols = slice(first * size, (first + 2) * size)
        do2 = do_ref[:, cols]
        x2 = x_ref[:, cols]
        parts = []
        for i in range(2):
            h = first + i
            half = slice(i * size, (i + 1) * size)
            decay = jnp.exp(cum_t_ref[:, h : h + 1] - cum_ref[h : h + 1, :] + same_ref[...])
            pair = dot(do2[:, half], x2[:, half], NT)
            weighted = decay * pair
            wsum[...] += weighted
            mixed = decay * cross
            parts.append(dot(mixed.astype(BF16), do2[:, half], TN))
            terms = (weighted * cross).astype(BF16)
            below = dot(upper, terms, NN)
            inner = jnp.sum(jnp.where(strict, below, 0.0), axis=1, keepdims=True)
            gl = jnp.where(lane == h, inner, gl)
        gx_ref[:, cols] = jnp.concatenate(parts, axis=1)
    gl_ref[...] = gl
    weighted = wsum[...].astype(BF16)
    gc_ref[...] = dot(weighted, b_ref[...], NN)
    gb_ref[...] = dot(weighted, c_ref[...], TN)

    def meet(own_u, own_w, own_a, level, bit):
        other_u = (got_u, got)[level][0].astype(F32)
        other_w = (got_u, got)[level][1].astype(F32)
        other_a = got_a[level, :1, :]
        later = bit.astype(F32)
        first = 1.0 - later
        sum_u = own_u * (later + first * other_a) + other_u * (first + later * own_a)
        sum_w = own_w * (first + later * other_a) + other_w * (later + first * own_a)
        return sum_u, sum_w, own_a * other_a, other_u, other_w, other_a, later, first

    for copy in exchange(0):
        copy.wait_recv()
    sum_u, sum_w, sum_a, other_u, other_w, other_a, later, first_in = meet(
        u_ref[0], u_ref[1], a_ref[:1, :], 0, odd
    )
    st_ref[0] = other_u * later
    st_ref[1] = other_w * first_in
    before_a = other_a * later + first_in
    after_a = other_a * first_in + later
    plane_sum[0] = sum_u
    plane_sum[1] = sum_w
    duo[0] = sum_u.astype(BF16)
    duo[1] = sum_w.astype(BF16)
    pair_a[...] = jnp.broadcast_to(sum_a, pair_a.shape)
    plane_a[1] = jnp.broadcast_to(before_a, pair_a.shape)
    plane_a[2] = jnp.broadcast_to(after_a, pair_a.shape)
    for copy in exchange(1):
        copy.start()

    for i in range(2):

        @pl.when(me - KWIN >= 0)
        def _():
            forward(0, i).wait_recv()

        @pl.when(side == 1)
        def _():
            forward(1, i).start()

        @pl.when(odd == 1)
        def _():
            forward(2, i).start()

    for i in range(2):
        forward(1, i).wait_recv()
        forward(3, i).start()
    for i in range(2):
        forward(2, i).wait_recv()
        forward(3, i).wait_recv()

    for copy in exchange(1):
        copy.wait_recv()
    sum_u, sum_w, sum_a, other_u, other_w, other_a, later, first_in = meet(
        plane_sum[0], plane_sum[1], pair_a[:1, :], 1, side
    )
    st_ref[0] = st_ref[0] + plane_a[1, :1, :] * later * other_u
    st_ref[1] = st_ref[1] + plane_a[2, :1, :] * first_in * other_w
    plane_a[1] = plane_a[1] * (other_a * later + first_in)
    plane_a[2] = plane_a[2] * (other_a * first_in + later)
    plane_a[0] = jnp.broadcast_to(sum_a, pair_a.shape)
    plane_sum[0] = sum_u
    plane_sum[1] = sum_w
    for i in range(2):
        chain_step(i, away[i] == 0)

    def pair_of_heads(step, carry):
        cols = pl.ds(pl.multiple_of(step * 2 * size, 2 * size), 2 * size)
        q2, do2 = q_ref[:, cols], do_ref[:, cols]
        k2, v2 = kw[:, cols], vw[:, cols]
        gq, gk, gv = [], [], []
        for i in range(2):
            half = slice(i * size, (i + 1) * size)
            qh, kh, vh, dh = q2[:, half], k2[:, half], v2[:, half], do2[:, half]
            e = jnp.exp(dot(qh, kh, NT) * scale + bias_ref[...])
            prob = e * (1.0 / jnp.sum(e, axis=1, keepdims=True))
            dprob = dot(dh, vh, NT)
            delta = jnp.sum(prob * dprob, axis=1, keepdims=True)
            ds = (prob * (dprob - delta) * scale).astype(BF16)
            gq.append(dot(ds, kh, NN))
            gk.append(dot(ds, qh, TN))
            gv.append(dot(prob.astype(BF16), dh, TN))
        gq_ref[:, cols] = jnp.concatenate(gq, axis=1).astype(BF16)
        pk[:, cols] = jnp.concatenate(gk, axis=1).astype(BF16)
        pv[:, cols] = jnp.concatenate(gv, axis=1).astype(BF16)
        return carry

    def add(i, c, slot, hop):
        cols = pl.ds(c * part, part)
        ref, got = (pk, pv)[i], (rk, rv)[i]
        ref[place(slot), cols] = (
            ref[place(slot), cols].astype(F32) + got[hop, :, cols].astype(F32)
        ).astype(BF16)

    def pass_across(c):
        for i in range(2):
            backward(3, i, c).wait_recv()
            add(i, c, 2, 3)
            backward(1, i, c).start()

    def pass_back(c):
        for i in range(2):
            backward(2, i, c).wait_recv()
            backward(1, i, c).wait_recv()
            cols = pl.ds(c * part, part)
            ref, got = (pk, pv)[i], (rk, rv)[i]
            near = got[2, :, cols].astype(F32)
            far = got[1, :, cols].astype(F32)
            near_own = (1 - odd).astype(F32)
            far_own = (1 - side).astype(F32)
            through = near * (1.0 - near_own) + far * (1.0 - far_own)
            kept = near * near_own + far * far_own
            ref[place(KWIN), cols] = (
                ref[place(KWIN), cols].astype(F32) + through
            ).astype(BF16)

            @pl.when(me - KWIN >= 0)
            def _():
                backward(0, i, c).start()

            total[i, :, cols] = ref[place(0), cols].astype(F32) + kept

    pairs = heads // 2 // PARTS
    for c in range(PARTS):
        lax.fori_loop(c * pairs, (c + 1) * pairs, pair_of_heads, 0)
        for hop in (3, 2):
            for i in range(2):
                backward(hop, i, c).start()
        if c > 0:
            pass_across(c - 1)
        else:
            for i in range(2):
                chain_step(i, away[i] == 1)
    pass_across(PARTS - 1)
    for c in range(PARTS):
        pass_back(c)
    for i in range(2):
        chain_step(i, away[i] > 1)
        st_ref[i] = st_ref[i] + plane_a[1 + i, :1, :] * chain_in[i]

    for i in range(2):

        @pl.when(me + KWIN < count)
        def _():
            forward(0, i).wait_send()
            for c in range(PARTS):
                cols = pl.ds(c * part, part)
                backward(0, i, c).wait_recv()
                total[i, :, cols] = total[i, :, cols] + (rk, rv)[i][0, :, cols].astype(F32)

        for hop in range(1, KWIN):
            forward(hop, i).wait_send()
            for c in range(PARTS):
                backward(hop, i, c).wait_send()

        @pl.when(me - KWIN >= 0)
        def _():
            for c in range(PARTS):
                backward(0, i, c).wait_send()

    for level in range(2):
        for copy in exchange(level):
            copy.wait_send()
    for i in range(2):

        @pl.when(away[1 - i] > 0)
        def _():
            chain_copy(i).wait_send()

    gk_ref[...] = total[0].astype(BF16)
    gv_ref[...] = total[1].astype(BF16)


def join_kernel(
    heads,
    states_ref,
    xl_ref,
    de_ref,
    leave_ref,
    b_ref,
    c_ref,
    through_ref,
    gxi_ref,
    gbi_ref,
    gci_ref,
    gli_ref,
    gx_ref,
    gb_ref,
    gc_ref,
    gl_ref,
):
    rows, width = gx_ref.shape
    size = width // heads
    lanes = gl_ref.shape[1]
    state, grad = states_ref[0], states_ref[1]
    state_b, grad_b = state.astype(BF16), grad.astype(BF16)
    state_f = (state - state_b.astype(F32)).astype(BF16)
    grad_f = (grad - grad_b.astype(F32)).astype(BF16)
    xl, de = xl_ref[...], de_ref[...]
    gc_ref[...] = (gci_ref[...] + dot(de, state_b, NT) + dot(de, state_f, NT)).astype(BF16)
    gb_ref[...] = (gbi_ref[...] + dot(xl, grad_b, NT) + dot(xl, grad_f, NT)).astype(BF16)
    back = dot(b_ref[...], grad_b, NN) + dot(b_ref[...], grad_f, NN)
    ahead = dot(c_ref[...], state_b, NN) + dot(c_ref[...], state_f, NN)
    gx_ref[...] = (gxi_ref[...] + leave_ref[...].astype(F32) * back).astype(BF16)
    owner = lax.broadcasted_iota(jnp.int32, (width, lanes), 0) // size
    pick = (owner == lax.broadcasted_iota(jnp.int32, (width, lanes), 1)).astype(F32)
    from_start = dot(de.astype(F32) * ahead, pick, NN, HIGH)
    to_end = dot(xl.astype(F32) * back, pick, NN, HIGH)
    row_id = lax.broadcasted_iota(jnp.int32, (rows, rows), 0)
    col_id = lax.broadcasted_iota(jnp.int32, (rows, rows), 1)
    later = dot((col_id >= row_id).astype(F32), from_start, NN, HIGH)
    earlier = dot((col_id < row_id).astype(F32), to_end, NN, HIGH)
    each = dot(jnp.ones((8, state.shape[0]), F32), grad * state, NN, HIGH)
    whole = dot(each, pick, NN, HIGH)[:1] * through_ref[...]
    gl_ref[...] = gli_ref[...] + later + earlier + whole


def body(
    queries,
    key_rows,
    value_rows,
    out_grad,
    ssm_input,
    state_write,
    state_read,
    log_decay,
    block_lists,
    rec_lengths,
):
    rows, width = queries.shape
    heads = log_decay.shape[0]
    size = width // heads
    states = state_write.shape[1]
    lanes = 128
    count = lax.axis_size("seq")
    me = lax.axis_index("seq")
    assert block_lists.shape[0] == 1

    ends = jnp.sum(
        jnp.where(
            jnp.arange(rec_lengths.shape[0])[:, None] >= jnp.arange(rec_lengths.shape[0])[None, :],
            rec_lengths[None, :],
            0,
        ),
        axis=1,
    )
    window = (me - KWIN) * rows + jnp.arange((KWIN + 1) * rows, dtype=jnp.int32)
    rec = jnp.sum((window[:, None] >= ends[None, :]).astype(jnp.int32), axis=1)
    own_pos, own_rec = window[KWIN * rows :], rec[KWIN * rows :]
    listed = jnp.any(block_lists[0][None, :] == (window // rows)[:, None], axis=1) & (window >= 0)
    allowed = (
        listed[None, :]
        & (rec[None, :] == own_rec[:, None])
        & (window[None, :] <= own_pos[:, None])
    )
    bias = jnp.where(allowed, 0.0, -1e30).astype(F32)
    same = jnp.where(
        (own_pos[:, None] >= own_pos[None, :]) & (own_rec[:, None] == own_rec[None, :]), 0.0, -1e30
    ).astype(F32)

    tri = (jnp.arange(rows)[:, None] <= jnp.arange(rows)[None, :]).astype(F32)
    cum = jnp.dot(log_decay, tri, precision=HIGH)
    first_keep = jnp.where(jnp.any(ends == own_pos[0]) | (own_pos[0] == 0), 0.0, 1.0)
    enter = jnp.exp(cum) * (first_keep * (own_rec == own_rec[0]).astype(F32))
    leave = jnp.exp(cum[:, -1:] - cum) * (own_rec == own_rec[-1]).astype(F32)
    through = enter[:, -1]
    leave_wide = jnp.repeat(leave.T, size, axis=1)
    enter_wide = jnp.repeat(enter.T, size, axis=1)
    xl = (ssm_input.astype(F32) * leave_wide).astype(BF16)
    de = (out_grad.astype(F32) * enter_wide).astype(BF16)
    ends_u = jnp.stack([dot(state_write, xl, TN), dot(state_read, de, TN)])
    ends_a = jnp.broadcast_to(enter_wide[-1:], (8, width))

    vmem = pl.BlockSpec(memory_space=pltpu.VMEM)
    wide = jax.ShapeDtypeStruct((rows, width), BF16)
    gq, gk, gv, gxi, gbi, gci, gli, joined = pl.pallas_call(
        functools.partial(mix_kernel, count, heads),
        out_shape=(
            wide,
            wide,
            wide,
            jax.ShapeDtypeStruct((rows, width), F32),
            jax.ShapeDtypeStruct((rows, states), F32),
            jax.ShapeDtypeStruct((rows, states), F32),
            jax.ShapeDtypeStruct((rows, lanes), F32),
            jax.ShapeDtypeStruct((2, states, width), F32),
        ),
        in_specs=[vmem] * 13,
        out_specs=(vmem,) * 8,
        scratch_shapes=[pltpu.VMEM(((KWIN + 1) * rows, width), BF16)] * 4
        + [pltpu.VMEM((KWIN, rows, width), BF16)] * 2
        + [pltpu.VMEM((rows, rows), F32), pltpu.VMEM((2, rows, width), F32)]
        + [
            pltpu.VMEM((2, states, width), F32),
            pltpu.VMEM((2, states, width), BF16),
            pltpu.VMEM((2, 8, width), F32),
            pltpu.VMEM((2, states, width), BF16),
            pltpu.VMEM((8, width), F32),
            pltpu.VMEM((2, states, width), F32),
            pltpu.VMEM((2, states, width), F32),
            pltpu.VMEM((2, states, width), F32),
            pltpu.VMEM((3, 8, width), F32),
        ]
        + [pltpu.SemaphoreType.DMA((3, 2))] * 2
        + [pltpu.SemaphoreType.DMA((KWIN, 2))] * 2
        + [pltpu.SemaphoreType.DMA((KWIN, 2 * PARTS))] * 2,
        compiler_params=pltpu.CompilerParams(
            collective_id=0, has_side_effects=True, vmem_limit_bytes=40 * 2**20
        ),
        cost_estimate=pl.CostEstimate(
            flops=10**10, bytes_accessed=3 * 10**7, transcendentals=10**6
        ),
    )(
        queries,
        key_rows,
        value_rows,
        out_grad,
        ssm_input,
        state_write,
        state_read,
        bias,
        same,
        cum,
        cum.T,
        ends_u,
        ends_a,
    )

    grad_input, grad_write, grad_read, grad_l = pl.pallas_call(
        functools.partial(join_kernel, heads),
        out_shape=(
            wide,
            jax.ShapeDtypeStruct((rows, states), BF16),
            jax.ShapeDtypeStruct((rows, states), BF16),
            jax.ShapeDtypeStruct((rows, lanes), F32),
        ),
        in_specs=[vmem] * 11,
        out_specs=(vmem,) * 4,
        compiler_params=pltpu.CompilerParams(vmem_limit_bytes=40 * 2**20),
    )(
        joined,
        xl,
        de,
        leave_wide,
        state_write,
        state_read,
        jnp.pad(through, (0, lanes - heads))[None],
        gxi,
        gbi,
        gci,
        gli,
    )
    return (gq, gk, gv, grad_input, grad_write, grad_read, grad_l[:, :heads].T)


def solution(mesh):
    rows = P(("grp", "seq"), None)
    turned = P(None, ("grp", "seq"))
    return jax.shard_map(
        body,
        mesh=mesh,
        in_specs=(rows,) * 7 + (turned, rows, P("grp")),
        out_specs=(rows,) * 6 + (turned,),
        check_vma=False,
    )
```

```python
import functools

import jax
import jax.numpy as jnp
from jax import lax
from jax.experimental import pallas as pl
from jax.experimental.pallas import tpu as pltpu
from jax.sharding import PartitionSpec as P

KWIN = 4
PARTS = 3
F32 = jnp.float32
BF16 = jnp.bfloat16
HIGH = lax.Precision.HIGHEST


def dot(a, b, dims, precision=None):
    return lax.dot_general(a, b, (dims, ((), ())), precision=precision, preferred_element_type=F32)


NN = ((1,), (0,))
NT = ((1,), (1,))
TN = ((0,), (0,))


def mix_kernel(
    count,
    heads,
    q_ref,
    k_ref,
    v_ref,
    do_ref,
    x_ref,
    b_ref,
    c_ref,
    bias_ref,
    same_ref,
    cum_ref,
    cum_t_ref,
    u_ref,
    a_ref,
    gq_ref,
    gk_ref,
    gv_ref,
    gx_ref,
    gb_ref,
    gc_ref,
    gl_ref,
    st_ref,
    kw,
    vw,
    pk,
    pv,
    rk,
    rv,
    wsum,
    total,
    got_u,
    got,
    got_a,
    duo,
    pair_a,
    chain,
    chain_in,
    plane_sum,
    plane_a,
    ssend_sem,
    srecv_sem,
    send_sem,
    recv_sem,
    bsend_sem,
    brecv_sem,
):
    me = lax.axis_index("seq")
    rows, width = q_ref.shape
    size = width // heads
    scale = size ** (-0.5)
    odd = lax.rem(me, 2)
    side = lax.div(lax.rem(me, KWIN), 2)
    mate = me + 1 - 2 * odd
    across = me + 2 - 4 * side
    part = width // PARTS

    def place(slot):
        return pl.ds(pl.multiple_of((KWIN - slot) * rows, rows), rows)

    routes = (
        (0, KWIN, me + KWIN),
        (KWIN * side, 2, across),
        (KWIN * odd, 1 + 2 * odd, mate),
        (2, 3 - 2 * odd, mate),
    )

    def forward(hop, i):
        src, dst, device = routes[hop]
        ref = (kw, vw)[i]
        return pltpu.make_async_remote_copy(
            src_ref=ref.at[place(src), :],
            dst_ref=ref.at[place(dst), :],
            send_sem=send_sem.at[hop, i],
            recv_sem=recv_sem.at[hop, i],
            device_id={"seq": device},
            device_id_type=pl.DeviceIdType.MESH,
        )

    backs = ((KWIN, me - KWIN), (2, across), (3 - 2 * odd, mate), (1 + 2 * odd, mate))

    def backward(hop, i, c):
        src, device = backs[hop]
        cols = pl.ds(c * part, part)
        return pltpu.make_async_remote_copy(
            src_ref=(pk, pv)[i].at[place(src), cols],
            dst_ref=(rk, rv)[i].at[hop, :, cols],
            send_sem=bsend_sem.at[hop, i * PARTS + c],
            recv_sem=brecv_sem.at[hop, i * PARTS + c],
            device_id={"seq": device},
            device_id_type=pl.DeviceIdType.MESH,
        )

    def state_copy(src, dst, device, level, i):
        return pltpu.make_async_remote_copy(
            src_ref=src,
            dst_ref=dst,
            send_sem=ssend_sem.at[level, i],
            recv_sem=srecv_sem.at[level, i],
            device_id={"seq": device},
            device_id_type=pl.DeviceIdType.MESH,
        )

    def exchange(level):
        src, src_a, device = ((u_ref, a_ref, mate), (duo, pair_a, across))[level]
        return (
            state_copy(src, (got_u, got)[level], device, level, 0),
            state_copy(src_a, got_a.at[level], device, level, 1),
        )

    def chain_copy(i):
        return state_copy(chain.at[i], chain_in.at[i], me + (KWIN, -KWIN)[i], 2, i)

    last = lax.div(count - 1, KWIN)
    plane = lax.div(me, KWIN)
    away = (plane, last - plane)

    def chain_step(i, now):
        @pl.when(now)
        def _():
            @pl.when(away[i] > 0)
            def _():
                chain_copy(i).wait_recv()

            @pl.when(away[1 - i] > 0)
            def _():
                chain[i] = (
                    plane_sum[i] + plane_a[0, :1, :] * chain_in[i]
                )
                chain_copy(i).start()

    barrier = pltpu.get_barrier_semaphore()
    for device in (mate, across):
        pl.semaphore_signal(
            barrier, inc=1, device_id={"seq": device}, device_id_type=pl.DeviceIdType.MESH
        )

    @pl.when(me + KWIN < count)
    def _():
        pl.semaphore_signal(
            barrier, inc=1, device_id={"seq": me + KWIN}, device_id_type=pl.DeviceIdType.MESH
        )

    @pl.when(me - KWIN >= 0)
    def _():
        pl.semaphore_signal(
            barrier, inc=1, device_id={"seq": me - KWIN}, device_id_type=pl.DeviceIdType.MESH
        )

    kw[place(0), :] = k_ref[...]
    vw[place(0), :] = v_ref[...]

    @pl.when(me < KWIN)
    def _():
        kw[place(KWIN), :] = jnp.zeros((rows, width), BF16)
        vw[place(KWIN), :] = jnp.zeros((rows, width), BF16)

    peers = 2 + (me + KWIN < count).astype(jnp.int32) + (me - KWIN >= 0).astype(jnp.int32)
    pl.semaphore_wait(barrier, peers)

    for copy in exchange(0):
        copy.start()

    for i in range(2):

        @pl.when(away[i] == 0)
        def _():
            chain_in[i] = jnp.zeros(chain_in.shape[1:], F32)

    for i in range(2):

        @pl.when(me + KWIN < count)
        def _():
            forward(0, i).start()

        @pl.when(side == 0)
        def _():
            forward(1, i).start()

        @pl.when(odd == 0)
        def _():
            forward(2, i).start()

    cross = dot(c_ref[...], b_ref[...], NT)
    row_id = lax.broadcasted_iota(jnp.int32, (rows, rows), 0)
    col_id = lax.broadcasted_iota(jnp.int32, (rows, rows), 1)
    upper = (col_id >= row_id).astype(BF16)
    strict = col_id < row_id
    lane = lax.broadcasted_iota(jnp.int32, (rows, gl_ref.shape[1]), 1)
    wsum[...] = jnp.zeros_like(wsum)
    gl = jnp.zeros(gl_ref.shape, F32)
    for first in range(0, heads, 2):
        cols = slice(first * size, (first + 2) * size)
        do2 = do_ref[:, cols]
        x2 = x_ref[:, cols]
        parts = []
        for i in range(2):
            h = first + i
            half = slice(i * size, (i + 1) * size)
            decay = jnp.exp(cum_t_ref[:, h : h + 1] - cum_ref[h : h + 1, :] + same_ref[...])
            pair = dot(do2[:, half], x2[:, half], NT)
            weighted = decay * pair
            wsum[...] += weighted
            mixed = decay * cross
            parts.append(dot(mixed.astype(BF16), do2[:, half], TN))
            terms = (weighted * cross).astype(BF16)
            below = dot(upper, terms, NN)
            inner = jnp.sum(jnp.where(strict, below, 0.0), axis=1, keepdims=True)
            gl = jnp.where(lane == h, inner, gl)
        gx_ref[:, cols] = jnp.concatenate(parts, axis=1)
    gl_ref[...] = gl
    weighted = wsum[...].astype(BF16)
    gc_ref[...] = dot(weighted, b_ref[...], NN)
    gb_ref[...] = dot(weighted, c_ref[...], TN)

    def meet(own_u, own_w, own_a, level, bit):
        other_u = (got_u, got)[level][0].astype(F32)
        other_w = (got_u, got)[level][1].astype(F32)
        other_a = got_a[level, :1, :]
        later = bit.astype(F32)
        first = 1.0 - later
        sum_u = own_u * (later + first * other_a) + other_u * (first + later * own_a)
        sum_w = own_w * (first + later * other_a) + other_w * (later + first * own_a)
        return sum_u, sum_w, own_a * other_a, other_u, other_w, other_a, later, first

    for copy in exchange(0):
        copy.wait_recv()
    sum_u, sum_w, sum_a, other_u, other_w, other_a, later, first_in = meet(
        u_ref[0], u_ref[1], a_ref[:1, :], 0, odd
    )
    st_ref[0] = other_u * later
    st_ref[1] = other_w * first_in
    before_a = other_a * later + first_in
    after_a = other_a * first_in + later
    plane_sum[0] = sum_u
    plane_sum[1] = sum_w
    duo[0] = sum_u.astype(BF16)
    duo[1] = sum_w.astype(BF16)
    pair_a[...] = jnp.broadcast_to(sum_a, pair_a.shape)
    plane_a[1] = jnp.broadcast_to(before_a, pair_a.shape)
    plane_a[2] = jnp.broadcast_to(after_a, pair_a.shape)
    for copy in exchange(1):
        copy.start()

    for i in range(2):

        @pl.when(me - KWIN >= 0)
        def _():
            forward(0, i).wait_recv()

        @pl.when(side == 1)
        def _():
            forward(1, i).start()

        @pl.when(odd == 1)
        def _():
            forward(2, i).start()

    for i in range(2):
        forward(1, i).wait_recv()
        forward(3, i).start()
    for i in range(2):
        forward(2, i).wait_recv()
        forward(3, i).wait_recv()

    for copy in exchange(1):
        copy.wait_recv()
    sum_u, sum_w, sum_a, other_u, other_w, other_a, later, first_in = meet(
        plane_sum[0], plane_sum[1], pair_a[:1, :], 1, side
    )
    st_ref[0] = st_ref[0] + plane_a[1, :1, :] * later * other_u
    st_ref[1] = st_ref[1] + plane_a[2, :1, :] * first_in * other_w
    plane_a[1] = plane_a[1] * (other_a * later + first_in)
    plane_a[2] = plane_a[2] * (other_a * first_in + later)
    plane_a[0] = jnp.broadcast_to(sum_a, pair_a.shape)
    plane_sum[0] = sum_u
    plane_sum[1] = sum_w
    for i in range(2):
        chain_step(i, away[i] == 0)

    def pair_of_heads(step, carry):
        cols = pl.ds(pl.multiple_of(step * 2 * size, 2 * size), 2 * size)
        q2, do2 = q_ref[:, cols], do_ref[:, cols]
        k2, v2 = kw[:, cols], vw[:, cols]
        gq, gk, gv = [], [], []
        for i in range(2):
            half = slice(i * size, (i + 1) * size)
            qh, kh, vh, dh = q2[:, half], k2[:, half], v2[:, half], do2[:, half]
            e = jnp.exp(dot(qh, kh, NT) * scale + bias_ref[...])
            prob = e * (1.0 / jnp.sum(e, axis=1, keepdims=True))
            dprob = dot(dh, vh, NT)
            delta = jnp.sum(prob * dprob, axis=1, keepdims=True)
            ds = (prob * (dprob - delta) * scale).astype(BF16)
            gq.append(dot(ds, kh, NN))
            gk.append(dot(ds, qh, TN))
            gv.append(dot(prob.astype(BF16), dh, TN))
        gq_ref[:, cols] = jnp.concatenate(gq, axis=1).astype(BF16)
        pk[:, cols] = jnp.concatenate(gk, axis=1).astype(BF16)
        pv[:, cols] = jnp.concatenate(gv, axis=1).astype(BF16)
        return carry

    def add(i, c, slot, hop):
        cols = pl.ds(c * part, part)
        ref, got = (pk, pv)[i], (rk, rv)[i]
        ref[place(slot), cols] = (
            ref[place(slot), cols].astype(F32) + got[hop, :, cols].astype(F32)
        ).astype(BF16)

    def pass_across(c):
        for i in range(2):
            backward(3, i, c).wait_recv()
            add(i, c, 2, 3)
            backward(1, i, c).start()

    def pass_back(c):
        for i in range(2):
            backward(2, i, c).wait_recv()
            backward(1, i, c).wait_recv()
            cols = pl.ds(c * part, part)
            ref, got = (pk, pv)[i], (rk, rv)[i]
            near = got[2, :, cols].astype(F32)
            far = got[1, :, cols].astype(F32)
            near_own = (1 - odd).astype(F32)
            far_own = (1 - side).astype(F32)
            through = near * (1.0 - near_own) + far * (1.0 - far_own)
            kept = near * near_own + far * far_own
            ref[place(KWIN), cols] = (
                ref[place(KWIN), cols].astype(F32) + through
            ).astype(BF16)

            @pl.when(me - KWIN >= 0)
            def _():
                backward(0, i, c).start()

            total[i, :, cols] = ref[place(0), cols].astype(F32) + kept

    pairs = heads // 2 // PARTS
    for c in range(PARTS):
        lax.fori_loop(c * pairs, (c + 1) * pairs, pair_of_heads, 0)
        for hop in (3, 2):
            for i in range(2):
                backward(hop, i, c).start()
        if c > 0:
            pass_across(c - 1)
        else:
            for i in range(2):
                chain_step(i, away[i] == 1)
    pass_across(PARTS - 1)
    for c in range(PARTS):
        pass_back(c)
    for i in range(2):
        chain_step(i, away[i] > 1)
        st_ref[i] = st_ref[i] + plane_a[1 + i, :1, :] * chain_in[i]

    for i in range(2):

        @pl.when(me + KWIN < count)
        def _():
            forward(0, i).wait_send()
            for c in range(PARTS):
                cols = pl.ds(c * part, part)
                backward(0, i, c).wait_recv()
                total[i, :, cols] = total[i, :, cols] + (rk, rv)[i][0, :, cols].astype(F32)

        for hop in range(1, KWIN):
            forward(hop, i).wait_send()
            for c in range(PARTS):
                backward(hop, i, c).wait_send()

        @pl.when(me - KWIN >= 0)
        def _():
            for c in range(PARTS):
                backward(0, i, c).wait_send()

    for level in range(2):
        for copy in exchange(level):
            copy.wait_send()
    for i in range(2):

        @pl.when(away[1 - i] > 0)
        def _():
            chain_copy(i).wait_send()

    gk_ref[...] = total[0].astype(BF16)
    gv_ref[...] = total[1].astype(BF16)


def join_kernel(
    heads,
    states_ref,
    xl_ref,
    de_ref,
    leave_ref,
    b_ref,
    c_ref,
    through_ref,
    gxi_ref,
    gbi_ref,
    gci_ref,
    gli_ref,
    gx_ref,
    gb_ref,
    gc_ref,
    gl_ref,
):
    rows, width = gx_ref.shape
    size = width // heads
    lanes = gl_ref.shape[1]
    state, grad = states_ref[0], states_ref[1]
    state_b, grad_b = state.astype(BF16), grad.astype(BF16)
    state_f = (state - state_b.astype(F32)).astype(BF16)
    grad_f = (grad - grad_b.astype(F32)).astype(BF16)
    xl, de = xl_ref[...], de_ref[...]
    gc_ref[...] = (gci_ref[...] + dot(de, state_b, NT) + dot(de, state_f, NT)).astype(BF16)
    gb_ref[...] = (gbi_ref[...] + dot(xl, grad_b, NT) + dot(xl, grad_f, NT)).astype(BF16)
    back = dot(b_ref[...], grad_b, NN) + dot(b_ref[...], grad_f, NN)
    ahead = dot(c_ref[...], state_b, NN) + dot(c_ref[...], state_f, NN)
    gx_ref[...] = (gxi_ref[...] + leave_ref[...].astype(F32) * back).astype(BF16)
    owner = lax.broadcasted_iota(jnp.int32, (width, lanes), 0) // size
    pick = (owner == lax.broadcasted_iota(jnp.int32, (width, lanes), 1)).astype(F32)
    from_start = dot(de.astype(F32) * ahead, pick, NN, HIGH)
    to_end = dot(xl.astype(F32) * back, pick, NN, HIGH)
    row_id = lax.broadcasted_iota(jnp.int32, (rows, rows), 0)
    col_id = lax.broadcasted_iota(jnp.int32, (rows, rows), 1)
    later = dot((col_id >= row_id).astype(F32), from_start, NN, HIGH)
    earlier = dot((col_id < row_id).astype(F32), to_end, NN, HIGH)
    each = dot(jnp.ones((8, state.shape[0]), F32), grad * state, NN, HIGH)
    whole = dot(each, pick, NN, HIGH)[:1] * through_ref[...]
    gl_ref[...] = gli_ref[...] + later + earlier + whole


def body(
    queries,
    key_rows,
    value_rows,
    out_grad,
    ssm_input,
    state_write,
    state_read,
    log_decay,
    block_lists,
    rec_lengths,
):
    rows, width = queries.shape
    heads = log_decay.shape[0]
    size = width // heads
    states = state_write.shape[1]
    lanes = 128
    count = lax.axis_size("seq")
    me = lax.axis_index("seq")
    assert block_lists.shape[0] == 1

    ends = jnp.sum(
        jnp.where(
            jnp.arange(rec_lengths.shape[0])[:, None] >= jnp.arange(rec_lengths.shape[0])[None, :],
            rec_lengths[None, :],
            0,
        ),
        axis=1,
    )
    window = (me - KWIN) * rows + jnp.arange((KWIN + 1) * rows, dtype=jnp.int32)
    rec = jnp.sum((window[:, None] >= ends[None, :]).astype(jnp.int32), axis=1)
    own_pos, own_rec = window[KWIN * rows :], rec[KWIN * rows :]
    listed = jnp.any(block_lists[0][None, :] == (window // rows)[:, None], axis=1) & (window >= 0)
    allowed = (
        listed[None, :]
        & (rec[None, :] == own_rec[:, None])
        & (window[None, :] <= own_pos[:, None])
    )
    bias = jnp.where(allowed, 0.0, -1e30).astype(F32)
    same = jnp.where(
        (own_pos[:, None] >= own_pos[None, :]) & (own_rec[:, None] == own_rec[None, :]), 0.0, -1e30
    ).astype(F32)

    tri = (jnp.arange(rows)[:, None] <= jnp.arange(rows)[None, :]).astype(F32)
    cum = jnp.dot(log_decay, tri, precision=HIGH)
    first_keep = jnp.where(jnp.any(ends == own_pos[0]) | (own_pos[0] == 0), 0.0, 1.0)
    enter = jnp.exp(cum) * (first_keep * (own_rec == own_rec[0]).astype(F32))
    leave = jnp.exp(cum[:, -1:] - cum) * (own_rec == own_rec[-1]).astype(F32)
    through = enter[:, -1]
    leave_wide = jnp.repeat(leave.T, size, axis=1)
    enter_wide = jnp.repeat(enter.T, size, axis=1)
    xl = (ssm_input.astype(F32) * leave_wide).astype(BF16)
    de = (out_grad.astype(F32) * enter_wide).astype(BF16)
    ends_u = jnp.stack([dot(state_write, xl, TN), dot(state_read, de, TN)])
    ends_a = jnp.broadcast_to(enter_wide[-1:], (8, width))

    vmem = pl.BlockSpec(memory_space=pltpu.VMEM)
    wide = jax.ShapeDtypeStruct((rows, width), BF16)
    gq, gk, gv, gxi, gbi, gci, gli, joined = pl.pallas_call(
        functools.partial(mix_kernel, count, heads),
        out_shape=(
            wide,
            wide,
            wide,
            jax.ShapeDtypeStruct((rows, width), F32),
            jax.ShapeDtypeStruct((rows, states), F32),
            jax.ShapeDtypeStruct((rows, states), F32),
            jax.ShapeDtypeStruct((rows, lanes), F32),
            jax.ShapeDtypeStruct((2, states, width), F32),
        ),
        in_specs=[vmem] * 13,
        out_specs=(vmem,) * 8,
        scratch_shapes=[pltpu.VMEM(((KWIN + 1) * rows, width), BF16)] * 4
        + [pltpu.VMEM((KWIN, rows, width), BF16)] * 2
        + [pltpu.VMEM((rows, rows), F32), pltpu.VMEM((2, rows, width), F32)]
        + [
            pltpu.VMEM((2, states, width), F32),
            pltpu.VMEM((2, states, width), BF16),
            pltpu.VMEM((2, 8, width), F32),
            pltpu.VMEM((2, states, width), BF16),
            pltpu.VMEM((8, width), F32),
            pltpu.VMEM((2, states, width), F32),
            pltpu.VMEM((2, states, width), F32),
            pltpu.VMEM((2, states, width), F32),
            pltpu.VMEM((3, 8, width), F32),
        ]
        + [pltpu.SemaphoreType.DMA((3, 2))] * 2
        + [pltpu.SemaphoreType.DMA((KWIN, 2))] * 2
        + [pltpu.SemaphoreType.DMA((KWIN, 2 * PARTS))] * 2,
        compiler_params=pltpu.CompilerParams(
            collective_id=0, has_side_effects=True, vmem_limit_bytes=40 * 2**20
        ),
        cost_estimate=pl.CostEstimate(
            flops=10**10, bytes_accessed=3 * 10**7, transcendentals=10**6
        ),
    )(
        queries,
        key_rows,
        value_rows,
        out_grad,
        ssm_input,
        state_write,
        state_read,
        bias,
        same,
        cum,
        cum.T,
        ends_u,
        ends_a,
    )

    grad_input, grad_write, grad_read, grad_l = pl.pallas_call(
        functools.partial(join_kernel, heads),
        out_shape=(
            wide,
            jax.ShapeDtypeStruct((rows, states), BF16),
            jax.ShapeDtypeStruct((rows, states), BF16),
            jax.ShapeDtypeStruct((rows, lanes), F32),
        ),
        in_specs=[vmem] * 11,
        out_specs=(vmem,) * 4,
        compiler_params=pltpu.CompilerParams(vmem_limit_bytes=40 * 2**20),
    )(
        joined,
        xl,
        de,
        leave_wide,
        state_write,
        state_read,
        jnp.pad(through, (0, lanes - heads))[None],
        gxi,
        gbi,
        gci,
        gli,
    )
    return (gq, gk, gv, grad_input, grad_write, grad_read, grad_l[:, :heads].T)


def solution(mesh):
    rows = P(("grp", "seq"), None)
    turned = P(None, ("grp", "seq"))
    return jax.shard_map(
        body,
        mesh=mesh,
        in_specs=(rows,) * 7 + (turned, rows, P("grp")),
        out_specs=(rows,) * 6 + (turned,),
        check_vma=False,
    )
```
